32 devices in a mesh: dp: 8 (over z, y), mp: 4 (over x, core).
Axes of the slice: x: 2, y: 2, z: 4, core: 2. Of those that a mesh axis runs over, the one named last changes fastest.
Arguments:
- features_in: bfloat16 [16, 24576], P(None, 'dp'), may hold values from -6 to 6
- w_in: bfloat16 [16, 1024], P(None, 'mp'), may hold values from -1.5 to 1.5
- w_mid: bfloat16 [1024, 1024], P(None, 'mp'), may hold values from -0.1875 to 0.1875
- w_out: bfloat16 [1024], P('mp'), may hold values from -0.1875 to 0.1875
- targets: float32 [24576], P('dp'), may hold values from -6 to 6
- valid_steps: int32 [256], P('dp'), may hold values from 16 to 96, as said below
Outputs:
- predicted_change: float32 [24576], P('dp')
The draws below stay inside these ranges and needn't reach their ends.
Inputs may be any that keep to these rules, and one draw needn't show every extreme that they name: `valid_steps`: the last building has all 96 valid steps.
All inputs are finite; a program needn't handle non-finite values.
Results may differ from the reference program's by a relative error of at most 0.00037.
Values may be sent and summed in bfloat16 or wider, within the bound.
A program may use at most 64 MiB of HBM per device.

```python
import jax
import jax.numpy as jnp
from jax import lax

H = 1024
F_IN = 16
STEPS = 96
ITERS = 3
B_DEV = 32
BUILDINGS = 256
ROWS = 24576
N_DP = 8


def draw_valid_steps(key, part):
    position = jnp.arange(BUILDINGS, dtype=jnp.int32)
    ceiling = STEPS // 3 + 2 * STEPS * (position + 1) // (3 * BUILDINGS)
    floor_value = ceiling // 2
    sampled = jax.random.randint(key, (BUILDINGS,), floor_value, ceiling + 1, dtype=jnp.int32)
    return jnp.where(position == BUILDINGS - 1, STEPS, sampled).astype(jnp.int32)


def steps_of(rng, shape, cuts, smallest, high):
    def one(dim, shards_of):
        heights = jax.random.uniform(jax.random.fold_in(jax.random.fold_in(rng, 6), dim), (shards_of,), jnp.float32, smallest / len(cuts), high / len(cuts))
        return jnp.repeat(jnp.exp(heights), shape[dim] // shards_of).reshape((-1,) + (1,) * (len(shape) - dim - 1))

    level = one(*cuts[0])
    for cut in cuts[1:]:
        level = level * one(*cut)
    return level


def scatter_about(rng, shape, spread, reach, cuts=(), kind=jnp.bfloat16):
    result = spread * jax.random.normal(rng, shape, jnp.float32)
    if cuts:
        result = result * steps_of(rng, shape, cuts, -0.22, 0.18)
    return jnp.clip(result, -reach, reach).astype(kind)


def setup_inputs(seed: int = 0) -> dict:
    key_list = jax.random.split(jax.random.key(seed), 7)
    return {
        "features_in": scatter_about(key_list[0], (F_IN, ROWS), 1.0, 6.0, ((1, 8),)),
        "w_in": scatter_about(key_list[1], (F_IN, H), F_IN ** -0.5, 1.5, ((1, 4),)),
        "w_mid": scatter_about(key_list[2], (H, H), H ** -0.5, 0.1875, ((1, 4),)),
        "w_out": scatter_about(key_list[3], (H,), H ** -0.5, 0.1875, ((0, 4),)),
        "targets": scatter_about(key_list[4], (ROWS,), 1.0, 6.0, ((0, 8),), jnp.float32),
        "valid_steps": draw_valid_steps(jax.random.fold_in(key_list[6], 71), 0),
    }


damping = 0.002


def reference(features_in, w_in, w_mid, w_out, targets, valid_steps):
    num_blocks = N_DP
    block_rows = B_DEV * STEPS
    feat_blocks = features_in.reshape(F_IN, num_blocks, block_rows).transpose(1, 0, 2)
    target_blocks = targets.reshape(num_blocks, block_rows)
    step_mask = (jnp.arange(STEPS, dtype=jnp.int32)[None, :] < valid_steps[:, None]).astype(jnp.float32)
    mask_blocks = step_mask.reshape(num_blocks, block_rows)
    valid_count = jnp.sum(valid_steps.astype(jnp.float32))
    out_weight = w_out.astype(jnp.float32)

    def layers(block_feat):
        hidden_one = jnp.tanh(jnp.dot(block_feat.T, w_in, preferred_element_type=jnp.float32)).astype(jnp.bfloat16)
        hidden_two = jnp.tanh(jnp.dot(hidden_one, w_mid, preferred_element_type=jnp.float32))
        slope_out = (1.0 - hidden_two * hidden_two) * out_weight
        return hidden_one, hidden_two, slope_out

    def grad_block(totals, block_item):
        block_feat, block_target, block_mask = block_item
        hidden_one, hidden_two, slope_out = layers(block_feat)
        predicted = jnp.sum(hidden_two * out_weight, axis=-1)
        error_rows = (block_mask / valid_count) * (predicted - block_target)
        grad_back = (error_rows[:, None] * slope_out).astype(jnp.bfloat16)
        return totals + jnp.dot(hidden_one.T, grad_back, preferred_element_type=jnp.float32), None

    gradient, _ = lax.scan(grad_block, jnp.zeros((H, H), jnp.float32), (feat_blocks, target_blocks, mask_blocks))

    def apply_curvature(vector):
        dir_bf16 = vector.astype(jnp.bfloat16)

        def curv_block(totals, block_item):
            block_feat, block_mask = block_item
            hidden_one, hidden_two, slope_out = layers(block_feat)
            tangent = jnp.sum(jnp.dot(hidden_one, dir_bf16, preferred_element_type=jnp.float32) * slope_out, axis=-1)
            back = (((block_mask / valid_count) * tangent)[:, None] * slope_out).astype(jnp.bfloat16)
            return totals + jnp.dot(hidden_one.T, back, preferred_element_type=jnp.float32), None

        summed, _ = lax.scan(curv_block, jnp.zeros((H, H), jnp.float32), (feat_blocks, mask_blocks))
        return summed + damping * vector

    solution = jnp.zeros((H, H), jnp.float32)
    remainder = -gradient
    direction = remainder
    norm_now = jnp.sum(remainder * remainder)
    for iteration in range(ITERS):
        curved = apply_curvature(direction)
        step_size = norm_now / jnp.sum(direction * curved)
        solution = solution + step_size * direction
        remainder = remainder - step_size * curved
        if iteration + 1 < ITERS:
            norm_next = jnp.sum(remainder * remainder)
            direction = remainder + (norm_next / norm_now) * direction
            norm_now = norm_next

    sol_bf16 = solution.astype(jnp.bfloat16)

    def change_block(carry, block_feat):
        hidden_one, hidden_two, slope_out = layers(block_feat)
        tangent = jnp.sum(jnp.dot(hidden_one, sol_bf16, preferred_element_type=jnp.float32) * slope_out, axis=-1)
        return carry, tangent

    _, changes = lax.scan(change_block, jnp.zeros((), jnp.float32), feat_blocks)
    return changes.reshape(-1)
```

```python
import functools

import jax
import jax.numpy as jnp
from jax import lax
from jax.experimental import pallas as pl
from jax.experimental.pallas import tpu as pltpu
from jax.sharding import PartitionSpec as P

STEPS = 96
damping = 0.002
MESH = pl.DeviceIdType.MESH
NT = (((1,), (1,)), ((), ()))
TN = (((0,), (0,)), ((), ()))


def tile_of(rows):
    return 512 if rows % 512 == 0 else 128


def kernel(
    nd, nm, feat, win, wmid, wout, targ, vs, out,
    win_all, h1t, st, ust, u_row, wmid_t, v_t, rows_out, rows_in, scal_out, scal_in,
    p_out, p_in, v_all, own, r_p, d_p, q_p,
    win_ss, win_rs, row_ss, row_rs, scal_ss, scal_rs, p_ss, p_rs, v_ss, v_rs,
):
    hidden, cols = wmid.shape
    rows = feat.shape[1]
    piece = hidden // nd
    tile = tile_of(rows)
    tiles = rows // tile
    dp = lax.axis_index("dp")
    mp = lax.axis_index("mp")

    barrier = pltpu.get_barrier_semaphore()

    @pl.loop(1, nd)
    def _(d):
        pl.semaphore_signal(
            barrier, inc=1, device_id=(lax.rem(dp + d, nd), mp), device_id_type=MESH
        )

    @pl.loop(1, nm)
    def _(d):
        pl.semaphore_signal(
            barrier, inc=1, device_id=(dp, lax.rem(mp + d, nm)), device_id_type=MESH
        )

    pl.semaphore_wait(barrier, nd - 1 + nm - 1)

    def win_copy(d):
        return pltpu.make_async_remote_copy(
            src_ref=win, dst_ref=win_all.at[d], send_sem=win_ss.at[d], recv_sem=win_rs.at[d],
            device_id=(dp, lax.rem(mp + d, nm)), device_id_type=MESH,
        )

    def row_copy(rnd, d):
        return pltpu.make_async_remote_copy(
            src_ref=rows_out.at[rnd], dst_ref=rows_in.at[rnd, d],
            send_sem=row_ss.at[rnd, d], recv_sem=row_rs.at[rnd, d],
            device_id=(dp, lax.rem(mp + d, nm)), device_id_type=MESH,
        )

    def scal_copy(rnd, d):
        return pltpu.make_async_remote_copy(
            src_ref=scal_out.at[rnd], dst_ref=scal_in.at[rnd, d],
            send_sem=scal_ss.at[rnd, d], recv_sem=scal_rs.at[rnd, d],
            device_id=(lax.rem(dp + d, nd), mp), device_id_type=MESH,
        )

    def p_copy(rnd, d):
        return pltpu.make_async_remote_copy(
            src_ref=p_out.at[rnd, d], dst_ref=p_in.at[rnd, d],
            send_sem=p_ss.at[rnd, d], recv_sem=p_rs.at[rnd, d],
            device_id=(lax.rem(dp + d, nd), mp), device_id_type=MESH,
        )

    def v_copy(rnd, d):
        mine = v_all.at[rnd, pl.ds(pl.multiple_of(dp * piece, piece), piece)]
        return pltpu.make_async_remote_copy(
            src_ref=mine, dst_ref=mine,
            send_sem=v_ss.at[rnd, d], recv_sem=v_rs.at[rnd, d],
            device_id=(lax.rem(dp + d, nd), mp), device_id_type=MESH,
        )

    def start(copy, n):
        @pl.loop(1, n)
        def _(d):
            copy(d).start()

    def finish(copy, n):
        @pl.loop(1, n)
        def _(d):
            copy(d).wait()

    def send_scalars(rnd, values):
        scal_out[rnd] = jnp.concatenate(
            [jnp.broadcast_to(v, (1, 128)) for v in values]
            + [jnp.zeros((8 - len(values), 128), jnp.float32)],
            axis=0,
        )
        start(functools.partial(scal_copy, rnd), nd)

    def sum_scalars(rnd):
        finish(functools.partial(scal_copy, rnd), nd)
        total = scal_out[rnd]
        for d in range(1, nd):
            total = total + scal_in[rnd, d]
        return total

    def sum_rows(rnd):
        start(functools.partial(row_copy, rnd), nm)
        finish(functools.partial(row_copy, rnd), nm)
        total = rows_out[rnd]
        for d in range(1, nm):
            total = total + rows_in[rnd, d]
        return total

    start(win_copy, nm)
    steps = vs[...]
    send_scalars(0, [jnp.sum(steps.astype(jnp.float32), axis=0, keepdims=True)])
    builds = vs.shape[0]
    offset = lax.broadcasted_iota(jnp.int32, (builds, rows), 1) - STEPS * (
        lax.broadcasted_iota(jnp.int32, (builds, rows), 0)
    )
    mask = jnp.sum(
        jnp.where((offset >= 0) & (offset < steps), 1.0, 0.0), axis=0, keepdims=True
    )
    wmid_t[...] = wmid[...].T
    win_all[0] = win[...]
    finish(win_copy, nm)

    @pl.loop(0, tiles)
    def _(i):
        at = pl.ds(pl.multiple_of(i * tile, tile), tile)
        block = feat[:, at]
        for d in range(nm):
            owner = lax.rem(mp + nm - d, nm)
            first = lax.dot_general(win_all[d], block, TN, preferred_element_type=jnp.float32)
            h1t[pl.ds(pl.multiple_of(owner * cols, cols), cols), at] = jnp.tanh(first).astype(
                jnp.bfloat16
            )
        two = jnp.tanh(jnp.dot(wmid_t[...], h1t[:, at], preferred_element_type=jnp.float32))
        weight = wout[...]
        st[:, at] = (1.0 - two * two) * weight
        rows_out[0, :, at] = jnp.sum(two * weight, axis=0, keepdims=True)

    def tangent(rnd):
        finish(functools.partial(v_copy, rnd), nd)
        v_t[...] = v_all[rnd].T

        @pl.loop(0, tiles)
        def _(i):
            at = pl.ds(pl.multiple_of(i * tile, tile), tile)
            z = jnp.dot(v_t[...], h1t[:, at], preferred_element_type=jnp.float32)
            rows_out[rnd + 1, :, at] = jnp.sum(z * st[:, at], axis=0, keepdims=True)

        return sum_rows(rnd + 1)

    def pull_back(rnd, row):
        u_row[...] = row

        @pl.loop(0, tiles)
        def _(i):
            at = pl.ds(pl.multiple_of(i * tile, tile), tile)
            ust[:, at] = (u_row[:, at] * st[:, at]).astype(jnp.bfloat16)

        def part(d):
            owner = lax.rem(dp + d, nd)
            left = h1t[pl.ds(pl.multiple_of(owner * piece, piece), piece), :]
            return lax.dot_general(left, ust[...], NT, preferred_element_type=jnp.float32)

        @pl.loop(1, nd)
        def _(d):
            p_out[rnd, d] = part(d).astype(jnp.bfloat16)
            p_copy(rnd, d).start()

        own[...] = part(0)
        finish(functools.partial(p_copy, rnd), nd)
        total = own[...]
        for d in range(1, nd):
            total = total + p_in[rnd, d].astype(jnp.float32)
        return total

    def spread(rnd):
        v_all[rnd, pl.ds(pl.multiple_of(dp * piece, piece), piece)] = r_p[...].astype(jnp.bfloat16)
        start(functools.partial(v_copy, rnd), nd)

    def dot(a, b):
        return jnp.sum(a * b, axis=1, keepdims=True)

    predicted = sum_rows(0)
    valid_count = sum_scalars(0)[0:1, 0:1]
    weight = mask / valid_count
    y_r = weight * (targ[...] - predicted)
    r_p[...] = pull_back(0, y_r)
    spread(0)
    t_r = tangent(0)
    wt = weight * t_r
    send_scalars(1, [dot(y_r, t_r), dot(wt, t_r)])
    q_p[...] = pull_back(1, wt)
    sums = sum_scalars(1)
    norm, curve = sums[0:1, 0:1], sums[1:2, 0:1]
    length = norm
    step = norm / (curve + damping * length)
    d_p[...] = r_p[...]
    r_p[...] = r_p[...] - step * (q_p[...] + damping * d_p[...])
    spread(1)
    t_d, y_d = t_r, y_r
    change = step * t_d
    y_r = y_r - step * (wt + damping * y_d)

    t_r = tangent(1)
    wt = weight * t_r
    send_scalars(2, [dot(y_r, t_r), dot(wt, t_r), dot(wt, t_d), dot(y_r, t_d)])
    back = pull_back(2, wt)
    sums = sum_scalars(2)
    beta = sums[0:1, 0:1] / norm
    norm = sums[0:1, 0:1]
    curve = sums[1:2, 0:1] + beta * (2.0 * sums[2:3, 0:1] + beta * curve)
    length = norm + beta * (2.0 * sums[3:4, 0:1] + beta * length)
    step = norm / (curve + damping * length)
    r_p[...] = r_p[...] - step * (
        back + beta * q_p[...] + damping * (r_p[...] + beta * d_p[...])
    )
    spread(2)
    t_d = t_r + beta * t_d
    y_d = y_r + beta * y_d
    change = change + step * t_d
    y_r = y_r - step * (weight * t_d + damping * y_d)

    t_r = tangent(2)
    wt = weight * t_r
    send_scalars(3, [dot(y_r, t_r), dot(wt, t_r), dot(wt, t_d), dot(y_r, t_d)])
    sums = sum_scalars(3)
    beta = sums[0:1, 0:1] / norm
    norm = sums[0:1, 0:1]
    curve = sums[1:2, 0:1] + beta * (2.0 * sums[2:3, 0:1] + beta * curve)
    length = norm + beta * (2.0 * sums[3:4, 0:1] + beta * length)
    step = norm / (curve + damping * length)
    t_d = t_r + beta * t_d
    out[...] = change + step * t_d


def shards(nd, nm, features_in, w_in, w_mid, w_out, targets, valid_steps):
    hidden, cols = w_mid.shape
    rows = features_in.shape[1]
    piece = hidden // nd
    vmem = pl.BlockSpec(memory_space=pltpu.VMEM)
    dma = pltpu.SemaphoreType.DMA
    bf16, f32 = jnp.bfloat16, jnp.float32
    change = pl.pallas_call(
        functools.partial(kernel, nd, nm),
        out_shape=jax.ShapeDtypeStruct((1, rows), f32),
        in_specs=[vmem] * 6,
        out_specs=vmem,
        scratch_shapes=[
            pltpu.VMEM((nm,) + w_in.shape, bf16),
            pltpu.VMEM((hidden, rows), bf16),
            pltpu.VMEM((cols, rows), f32),
            pltpu.VMEM((cols, rows), bf16),
            pltpu.VMEM((1, rows), f32),
            pltpu.VMEM((cols, hidden), bf16),
            pltpu.VMEM((cols, hidden), bf16),
            pltpu.VMEM((4, 1, rows), f32),
            pltpu.VMEM((4, nm, 1, rows), f32),
            pltpu.VMEM((4, 8, 128), f32),
            pltpu.VMEM((4, nd, 8, 128), f32),
            pltpu.VMEM((3, nd, piece, cols), bf16),
            pltpu.VMEM((3, nd, piece, cols), bf16),
            pltpu.VMEM((3, hidden, cols), bf16),
            pltpu.VMEM((piece, cols), f32),
            pltpu.VMEM((piece, cols), f32),
            pltpu.VMEM((piece, cols), f32),
            pltpu.VMEM((piece, cols), f32),
            dma((nm,)), dma((nm,)),
            dma((4, nm)), dma((4, nm)),
            dma((4, nd)), dma((4, nd)),
            dma((3, nd)), dma((3, nd)),
            dma((3, nd)), dma((3, nd)),
        ],
        compiler_params=pltpu.CompilerParams(
            collective_id=0, has_side_effects=True, vmem_limit_bytes=56 * 1024 * 1024
        ),
    )(
        features_in,
        w_in,
        w_mid,
        w_out.astype(f32).reshape(cols, 1),
        targets.reshape(1, rows),
        valid_steps.reshape(-1, 1),
    )
    return change.reshape(rows)


def solution(mesh):
    return jax.shard_map(
        functools.partial(shards, mesh.shape["dp"], mesh.shape["mp"]),
        mesh=mesh,
        in_specs=(P(None, "dp"), P(None, "mp"), P(None, "mp"), P("mp"), P("dp"), P("dp")),
        out_specs=P("dp"),
        check_vma=False,
    )
```

```python
import functools

import jax
import jax.numpy as jnp
from jax import lax
from jax.experimental import pallas as pl
from jax.experimental.pallas import tpu as pltpu
from jax.sharding import PartitionSpec as P

STEPS = 96
damping = 0.002
MESH = pl.DeviceIdType.MESH
NT = (((1,), (1,)), ((), ()))


def tile_of(rows):
    return 512 if rows % 512 == 0 else 128


def kernel(
    nd, nm, feat, win, wmid, wout, targ, vs, out,
    win_all, win_t, h1t, st, ust, u_row, wmid_t, v_t, rows_out, rows_in, scal_out, scal_in,
    y_out, y_in, z_out, z_in, v_all, r_p, d_p, q_p,
    win_ss, win_rs, row_ss, row_rs, scal_ss, scal_rs,
    y_ss, y_rs, z_ss, z_rs, vy_ss, vy_rs, vz_ss, vz_rs,
):
    hidden, cols = wmid.shape
    rows = feat.shape[1]
    piece = hidden // nd
    tile = tile_of(rows)
    tiles = rows // tile
    dp = lax.axis_index("dp")
    mp = lax.axis_index("mp")
    nz = nd // 2
    z, y = dp // 2, lax.rem(dp, 2)

    def rows_of(z_at, y_at):
        return pl.ds(pl.multiple_of((y_at * nz + z_at) * piece, piece), piece)

    barrier = pltpu.get_barrier_semaphore()

    @pl.loop(1, nd)
    def _(d):
        pl.semaphore_signal(
            barrier, inc=1, device_id=(lax.rem(dp + d, nd), mp), device_id_type=MESH
        )

    @pl.loop(1, nm)
    def _(d):
        pl.semaphore_signal(
            barrier, inc=1, device_id=(dp, lax.rem(mp + d, nm)), device_id_type=MESH
        )

    pl.semaphore_wait(barrier, nd - 1 + nm - 1)

    def win_copy(d):
        return pltpu.make_async_remote_copy(
            src_ref=win, dst_ref=win_all.at[d], send_sem=win_ss.at[d], recv_sem=win_rs.at[d],
            device_id=(dp, lax.rem(mp + d, nm)), device_id_type=MESH,
        )

    def row_copy(rnd, d):
        return pltpu.make_async_remote_copy(
            src_ref=rows_out.at[rnd], dst_ref=rows_in.at[rnd, d],
            send_sem=row_ss.at[rnd, d], recv_sem=row_rs.at[rnd, d],
            device_id=(dp, lax.rem(mp + d, nm)), device_id_type=MESH,
        )

    def scal_copy(rnd, d):
        return pltpu.make_async_remote_copy(
            src_ref=scal_out.at[rnd], dst_ref=scal_in.at[rnd, d],
            send_sem=scal_ss.at[rnd, d], recv_sem=scal_rs.at[rnd, d],
            device_id=(lax.rem(dp + d, nd), mp), device_id_type=MESH,
        )

    def y_copy(rnd, d):
        return pltpu.make_async_remote_copy(
            src_ref=y_out.at[rnd, d], dst_ref=y_in.at[rnd, d],
            send_sem=y_ss.at[rnd, d], recv_sem=y_rs.at[rnd, d],
            device_id=(z * 2 + 1 - y, mp), device_id_type=MESH,
        )

    def z_copy(rnd, d):
        return pltpu.make_async_remote_copy(
            src_ref=z_out.at[rnd, d], dst_ref=z_in.at[rnd, d],
            send_sem=z_ss.at[rnd, d], recv_sem=z_rs.at[rnd, d],
            device_id=(lax.rem(z + d, nz) * 2 + y, mp), device_id_type=MESH,
        )

    def vz_copy(rnd, d):
        mine = v_all.at[rnd, rows_of(z, y)]
        return pltpu.make_async_remote_copy(
            src_ref=mine, dst_ref=mine,
            send_sem=vz_ss.at[rnd, d], recv_sem=vz_rs.at[rnd, d],
            device_id=(lax.rem(z + d, nz) * 2 + y, mp), device_id_type=MESH,
        )

    def vy_copy(rnd, d):
        theirs = v_all.at[rnd, rows_of(lax.rem(z + nz - d, nz), y)]
        return pltpu.make_async_remote_copy(
            src_ref=theirs, dst_ref=theirs,
            send_sem=vy_ss.at[rnd, d], recv_sem=vy_rs.at[rnd, d],
            device_id=(z * 2 + 1 - y, mp), device_id_type=MESH,
        )

    def start(copy, n):
        @pl.loop(1, n)
        def _(d):
            copy(d).start()

    def finish(copy, n):
        @pl.loop(1, n)
        def _(d):
            copy(d).wait()

    def send_scalars(rnd, values):
        scal_out[rnd] = jnp.concatenate(
            [jnp.broadcast_to(v, (1, 128)) for v in values]
            + [jnp.zeros((8 - len(values), 128), jnp.float32)],
            axis=0,
        )
        start(functools.partial(scal_copy, rnd), nd)

    def sum_scalars(rnd):
        finish(functools.partial(scal_copy, rnd), nd)
        total = scal_out[rnd]
        for d in range(1, nd):
            total = total + scal_in[rnd, d]
        return total

    def sum_rows(rnd):
        start(functools.partial(row_copy, rnd), nm)
        finish(functools.partial(row_copy, rnd), nm)
        total = rows_out[rnd]
        for d in range(1, nm):
            total = total + rows_in[rnd, d]
        return total

    start(win_copy, nm)
    steps = vs[...]
    send_scalars(0, [jnp.sum(steps.astype(jnp.float32), axis=0, keepdims=True)])
    builds = vs.shape[0]
    offset = lax.broadcasted_iota(jnp.int32, (builds, rows), 1) - STEPS * (
        lax.broadcasted_iota(jnp.int32, (builds, rows), 0)
    )
    mask = jnp.sum(
        jnp.where((offset >= 0) & (offset < steps), 1.0, 0.0), axis=0, keepdims=True
    )
    wmid_t[...] = wmid[...].T
    win_all[0] = win[...]
    finish(win_copy, nm)
    for d in range(nm):
        owner = lax.rem(mp + nm - d, nm)
        win_t[pl.ds(pl.multiple_of(owner * cols, cols), cols), :] = win_all[d].T

    @pl.loop(0, tiles)
    def _(i):
        at = pl.ds(pl.multiple_of(i * tile, tile), tile)
        block = feat[:, at]
        first = jnp.dot(win_t[...], block, preferred_element_type=jnp.float32)
        h1t[:, at] = jnp.tanh(first).astype(jnp.bfloat16)
        two = jnp.tanh(jnp.dot(wmid_t[...], h1t[:, at], preferred_element_type=jnp.float32))
        weight = wout[...]
        st[:, at] = (1.0 - two * two) * weight
        rows_out[0, :, at] = jnp.sum(two * weight, axis=0, keepdims=True)

    def tangent(rnd):
        @pl.loop(1, nz)
        def _(d):
            vz_copy(rnd, d).wait_recv()
            vy_copy(rnd, d).start()

        @pl.loop(0, nz)
        def _(d):
            vy_copy(rnd, d).wait()

        @pl.loop(1, nz)
        def _(d):
            vz_copy(rnd, d).wait_send()

        v_t[...] = v_all[rnd].T

        @pl.loop(0, tiles)
        def _(i):
            at = pl.ds(pl.multiple_of(i * tile, tile), tile)
            z = jnp.dot(v_t[...], h1t[:, at], preferred_element_type=jnp.float32)
            rows_out[rnd + 1, :, at] = jnp.sum(z * st[:, at], axis=0, keepdims=True)

        return sum_rows(rnd + 1)

    def pull_back(rnd, row):
        u_row[...] = row

        @pl.loop(0, tiles)
        def _(i):
            at = pl.ds(pl.multiple_of(i * tile, tile), tile)
            ust[:, at] = (u_row[:, at] * st[:, at]).astype(jnp.bfloat16)

        def part(z_at, y_at):
            left = h1t[rows_of(z_at, y_at), :]
            return lax.dot_general(left, ust[...], NT, preferred_element_type=jnp.float32)

        @pl.loop(1, nz + 1)
        def _(i):
            d = lax.rem(i, nz)
            y_out[rnd, d] = part(lax.rem(z + d, nz), 1 - y).astype(jnp.bfloat16)
            y_copy(rnd, d).start()

        @pl.loop(1, nz)
        def _(d):
            mine = part(lax.rem(z + d, nz), y)
            y_copy(rnd, d).wait_recv()
            z_out[rnd, d] = (mine + y_in[rnd, d].astype(jnp.float32)).astype(jnp.bfloat16)
            z_copy(rnd, d).start()

        total = part(z, y)
        y_copy(rnd, 0).wait_recv()
        total = total + y_in[rnd, 0].astype(jnp.float32)
        finish(functools.partial(z_copy, rnd), nz)
        for d in range(1, nz):
            total = total + z_in[rnd, d].astype(jnp.float32)

        @pl.loop(0, nz)
        def _(d):
            y_copy(rnd, d).wait_send()

        return total

    def spread(rnd):
        v_all[rnd, rows_of(z, y)] = r_p[...].astype(jnp.bfloat16)
        start(functools.partial(vz_copy, rnd), nz)
        vy_copy(rnd, 0).start()

    def dot(a, b):
        return jnp.sum(a * b, axis=1, keepdims=True)

    predicted = sum_rows(0)
    valid_count = sum_scalars(0)[0:1, 0:1]
    weight = mask / valid_count
    y_r = weight * (targ[...] - predicted)
    r_p[...] = pull_back(0, y_r)
    spread(0)
    t_r = tangent(0)
    wt = weight * t_r
    send_scalars(1, [dot(y_r, t_r), dot(wt, t_r)])
    q_p[...] = pull_back(1, wt)
    sums = sum_scalars(1)
    norm, curve = sums[0:1, 0:1], sums[1:2, 0:1]
    length = norm
    step = norm / (curve + damping * length)
    d_p[...] = r_p[...]
    r_p[...] = r_p[...] - step * (q_p[...] + damping * d_p[...])
    spread(1)
    t_d, y_d = t_r, y_r
    change = step * t_d
    y_r = y_r - step * (wt + damping * y_d)

    t_r = tangent(1)
    wt = weight * t_r
    send_scalars(2, [dot(y_r, t_r), dot(wt, t_r), dot(wt, t_d), dot(y_r, t_d)])
    back = pull_back(2, wt)
    sums = sum_scalars(2)
    beta = sums[0:1, 0:1] / norm
    norm = sums[0:1, 0:1]
    curve = sums[1:2, 0:1] + beta * (2.0 * sums[2:3, 0:1] + beta * curve)
    length = norm + beta * (2.0 * sums[3:4, 0:1] + beta * length)
    step = norm / (curve + damping * length)
    r_p[...] = r_p[...] - step * (
        back + beta * q_p[...] + damping * (r_p[...] + beta * d_p[...])
    )
    spread(2)
    t_d = t_r + beta * t_d
    y_d = y_r + beta * y_d
    change = change + step * t_d
    y_r = y_r - step * (weight * t_d + damping * y_d)

    t_r = tangent(2)
    wt = weight * t_r
    send_scalars(3, [dot(y_r, t_r), dot(wt, t_r), dot(wt, t_d), dot(y_r, t_d)])
    sums = sum_scalars(3)
    beta = sums[0:1, 0:1] / norm
    norm = sums[0:1, 0:1]
    curve = sums[1:2, 0:1] + beta * (2.0 * sums[2:3, 0:1] + beta * curve)
    length = norm + beta * (2.0 * sums[3:4, 0:1] + beta * length)
    step = norm / (curve + damping * length)
    t_d = t_r + beta * t_d
    out[...] = change + step * t_d


def shards(nd, nm, features_in, w_in, w_mid, w_out, targets, valid_steps):
    hidden, cols = w_mid.shape
    rows = features_in.shape[1]
    piece = hidden // nd
    vmem = pl.BlockSpec(memory_space=pltpu.VMEM)
    dma = pltpu.SemaphoreType.DMA
    bf16, f32 = jnp.bfloat16, jnp.float32
    change = pl.pallas_call(
        functools.partial(kernel, nd, nm),
        out_shape=jax.ShapeDtypeStruct((1, rows), f32),
        in_specs=[vmem] * 6,
        out_specs=vmem,
        scratch_shapes=[
            pltpu.VMEM((nm,) + w_in.shape, bf16),
            pltpu.VMEM((hidden, w_in.shape[0]), bf16),
            pltpu.VMEM((hidden, rows), bf16),
            pltpu.VMEM((cols, rows), f32),
            pltpu.VMEM((cols, rows), bf16),
            pltpu.VMEM((1, rows), f32),
            pltpu.VMEM((cols, hidden), bf16),
            pltpu.VMEM((cols, hidden), bf16),
            pltpu.VMEM((4, 1, rows), f32),
            pltpu.VMEM((4, nm, 1, rows), f32),
            pltpu.VMEM((4, 8, 128), f32),
            pltpu.VMEM((4, nd, 8, 128), f32),
            pltpu.VMEM((3, nd // 2, piece, cols), bf16),
            pltpu.VMEM((3, nd // 2, piece, cols), bf16),
            pltpu.VMEM((3, nd // 2, piece, cols), bf16),
            pltpu.VMEM((3, nd // 2, piece, cols), bf16),
            pltpu.VMEM((3, hidden, cols), bf16),
            pltpu.VMEM((piece, cols), f32),
            pltpu.VMEM((piece, cols), f32),
            pltpu.VMEM((piece, cols), f32),
            dma((nm,)), dma((nm,)),
            dma((4, nm)), dma((4, nm)),
            dma((4, nd)), dma((4, nd)),
            dma((3, nd // 2)), dma((3, nd // 2)),
            dma((3, nd // 2)), dma((3, nd // 2)),
            dma((3, nd // 2)), dma((3, nd // 2)),
            dma((3, nd // 2)), dma((3, nd // 2)),
        ],
        compiler_params=pltpu.CompilerParams(
            collective_id=0, has_side_effects=True, vmem_limit_bytes=56 * 1024 * 1024
        ),
    )(
        features_in,
        w_in,
        w_mid,
        w_out.astype(f32).reshape(cols, 1),
        targets.reshape(1, rows),
        valid_steps.reshape(-1, 1),
    )
    return change.reshape(rows)


def solution(mesh):
    return jax.shard_map(
        functools.partial(shards, mesh.shape["dp"], mesh.shape["mp"]),
        mesh=mesh,
        in_specs=(P(None, "dp"), P(None, "mp"), P(None, "mp"), P("mp"), P("dp"), P("dp")),
        out_specs=P("dp"),
        check_vma=False,
    )
```

```python
import functools

import jax
import jax.numpy as jnp
from jax import lax
from jax.experimental import pallas as pl
from jax.experimental.pallas import tpu as pltpu
from jax.sharding import PartitionSpec as P

STEPS = 96
damping = 0.002
MESH = pl.DeviceIdType.MESH
NT = (((1,), (1,)), ((), ()))


def tile_of(rows):
    return 512 if rows % 512 == 0 else 128


def upright(row):
    n = row.shape[1]
    here = lax.broadcasted_iota(jnp.int32, (n, n), 0) == lax.broadcasted_iota(
        jnp.int32, (n, n), 1
    )
    return jnp.sum(jnp.where(here, row, 0.0), axis=1, keepdims=True)


def kernel(
    nd, nm, feat, win, wmid, wout, targ, vs, out,
    win_all, win_t, h1t, st, ust, u_row, wmid_t, v_t, rows_out, rows_in, scal_out, scal_in,
    y_out, y_in, z_out, z_in, v_all, r_p, d_p, q_p,
    win_ss, win_rs, row_ss, row_rs, scal_ss, scal_rs,
    y_ss, y_rs, z_ss, z_rs, vy_ss, vy_rs, hop_ss, hop_rs,
):
    hidden, cols = wmid.shape
    rows = feat.shape[1]
    piece = hidden // nd
    tile = tile_of(rows)
    tiles = rows // tile
    dp = lax.axis_index("dp")
    mp = lax.axis_index("mp")
    nz = nd // 2
    z, y = dp // 2, lax.rem(dp, 2)

    def rows_of(z_at, y_at):
        return pl.ds(pl.multiple_of((y_at * nz + z_at) * piece, piece), piece)

    barrier = pltpu.get_barrier_semaphore()

    @pl.loop(1, nd)
    def _(d):
        pl.semaphore_signal(
            barrier, inc=1, device_id=(lax.rem(dp + d, nd), mp), device_id_type=MESH
        )

    @pl.loop(1, nm)
    def _(d):
        pl.semaphore_signal(
            barrier, inc=1, device_id=(dp, lax.rem(mp + d, nm)), device_id_type=MESH
        )

    pl.semaphore_wait(barrier, nd - 1 + nm - 1)

    def win_copy(d):
        return pltpu.make_async_remote_copy(
            src_ref=win, dst_ref=win_all.at[d], send_sem=win_ss.at[d], recv_sem=win_rs.at[d],
            device_id=(dp, lax.rem(mp + d, nm)), device_id_type=MESH,
        )

    def row_copy(rnd, d):
        return pltpu.make_async_remote_copy(
            src_ref=rows_out.at[rnd], dst_ref=rows_in.at[rnd, d],
            send_sem=row_ss.at[rnd, d], recv_sem=row_rs.at[rnd, d],
            device_id=(dp, lax.rem(mp + d, nm)), device_id_type=MESH,
        )

    def scal_copy(rnd, d):
        return pltpu.make_async_remote_copy(
            src_ref=scal_out.at[rnd], dst_ref=scal_in.at[rnd, d],
            send_sem=scal_ss.at[rnd, d], recv_sem=scal_rs.at[rnd, d],
            device_id=(lax.rem(dp + d, nd), mp), device_id_type=MESH,
        )

    def y_copy(rnd, d):
        return pltpu.make_async_remote_copy(
            src_ref=y_out.at[rnd, d], dst_ref=y_in.at[rnd, d],
            send_sem=y_ss.at[rnd, d], recv_sem=y_rs.at[rnd, d],
            device_id=(z * 2 + 1 - y, mp), device_id_type=MESH,
        )

    def z_copy(rnd, d):
        return pltpu.make_async_remote_copy(
            src_ref=z_out.at[rnd, d], dst_ref=z_in.at[rnd, d],
            send_sem=z_ss.at[rnd, d], recv_sem=z_rs.at[rnd, d],
            device_id=(lax.rem(z + d, nz) * 2 + y, mp), device_id_type=MESH,
        )

    def hop_copy(rnd, way, owner):
        block = v_all.at[rnd, rows_of(owner, y)]
        z_to = lax.rem(z + 1, nz) if way == 0 else lax.rem(z + nz - 1, nz)
        return pltpu.make_async_remote_copy(
            src_ref=block, dst_ref=block,
            send_sem=hop_ss.at[rnd, way, owner], recv_sem=hop_rs.at[rnd, way, owner],
            device_id=(z_to * 2 + y, mp), device_id_type=MESH,
        )

    def vy_copy(rnd, owner):
        block = v_all.at[rnd, rows_of(owner, y)]
        return pltpu.make_async_remote_copy(
            src_ref=block, dst_ref=block,
            send_sem=vy_ss.at[rnd, owner], recv_sem=vy_rs.at[rnd, owner],
            device_id=(z * 2 + 1 - y, mp), device_id_type=MESH,
        )

    def pass_on(rnd, owner):
        @pl.when((owner <= z) & (z + 1 < nz))
        def _():
            hop_copy(rnd, 0, owner).start()

        @pl.when((owner >= z) & (z > 0))
        def _():
            hop_copy(rnd, 1, owner).start()

        vy_copy(rnd, owner).start()

    def start(copy, n):
        @pl.loop(1, n)
        def _(d):
            copy(d).start()

    def finish(copy, n):
        @pl.loop(1, n)
        def _(d):
            copy(d).wait()

    def send_scalars(rnd, values):
        scal_out[rnd] = jnp.concatenate(
            [jnp.broadcast_to(v, (1, 128)) for v in values]
            + [jnp.zeros((8 - len(values), 128), jnp.float32)],
            axis=0,
        )
        start(functools.partial(scal_copy, rnd), nd)

    def sum_scalars(rnd):
        finish(functools.partial(scal_copy, rnd), nd)
        total = scal_out[rnd]
        for d in range(1, nd):
            total = total + scal_in[rnd, d]
        return total

    def sum_rows(rnd):
        start(functools.partial(row_copy, rnd), nm)
        finish(functools.partial(row_copy, rnd), nm)
        total = rows_out[rnd]
        for d in range(1, nm):
            total = total + rows_in[rnd, d]
        return total

    start(win_copy, nm)
    steps = upright(vs[...].astype(jnp.float32))
    out_weight = upright(wout[...].astype(jnp.float32))
    send_scalars(0, [jnp.sum(steps, axis=0, keepdims=True)])
    builds = vs.shape[1]
    offset = lax.broadcasted_iota(jnp.int32, (builds, rows), 1) - STEPS * (
        lax.broadcasted_iota(jnp.int32, (builds, rows), 0)
    )
    mask = jnp.sum(
        jnp.where((offset >= 0) & (offset.astype(jnp.float32) < steps), 1.0, 0.0), axis=0, keepdims=True
    )
    wmid_t[...] = wmid[...].T
    win_all[0] = win[...]
    finish(win_copy, nm)
    for d in range(nm):
        owner = lax.rem(mp + nm - d, nm)
        win_t[pl.ds(pl.multiple_of(owner * cols, cols), cols), :] = win_all[d].T

    @pl.loop(0, tiles)
    def _(i):
        at = pl.ds(pl.multiple_of(i * tile, tile), tile)
        block = feat[:, at]
        first = jnp.dot(win_t[...], block, preferred_element_type=jnp.float32)
        h1t[:, at] = jnp.tanh(first).astype(jnp.bfloat16)
        two = jnp.tanh(jnp.dot(wmid_t[...], h1t[:, at], preferred_element_type=jnp.float32))
        weight = out_weight
        st[:, at] = (1.0 - two * two) * weight
        rows_out[0, :, at] = jnp.sum(two * weight, axis=0, keepdims=True)

    def tangent(rnd):
        @pl.loop(1, nz)
        def _(d):
            @pl.when(z - d >= 0)
            def _():
                hop_copy(rnd, 0, z - d).wait_recv()
                pass_on(rnd, z - d)

            @pl.when(z + d < nz)
            def _():
                hop_copy(rnd, 1, z + d).wait_recv()
                pass_on(rnd, z + d)

        half = hidden // 2
        near = pl.ds(pl.multiple_of(y * half, half), half)
        far = pl.ds(pl.multiple_of((1 - y) * half, half), half)
        v_t[:, near] = v_all[rnd, near].T

        @pl.loop(0, nz)
        def _(owner):
            vy_copy(rnd, owner).wait()

            @pl.when((owner <= z) & (z + 1 < nz))
            def _():
                hop_copy(rnd, 0, owner).wait_send()

            @pl.when((owner >= z) & (z > 0))
            def _():
                hop_copy(rnd, 1, owner).wait_send()

        v_t[:, far] = v_all[rnd, far].T

        @pl.loop(0, tiles)
        def _(i):
            at = pl.ds(pl.multiple_of(i * tile, tile), tile)
            z = jnp.dot(v_t[...], h1t[:, at], preferred_element_type=jnp.float32)
            rows_out[rnd + 1, :, at] = jnp.sum(z * st[:, at], axis=0, keepdims=True)

        return sum_rows(rnd + 1)

    def pull_back(rnd, row):
        u_row[...] = row

        @pl.loop(0, tiles)
        def _(i):
            at = pl.ds(pl.multiple_of(i * tile, tile), tile)
            ust[:, at] = (u_row[:, at] * st[:, at]).astype(jnp.bfloat16)

        def part(z_at, y_at):
            left = h1t[rows_of(z_at, y_at), :]
            return lax.dot_general(left, ust[...], NT, preferred_element_type=jnp.float32)

        @pl.loop(1, nz + 1)
        def _(i):
            d = lax.rem(i, nz)
            y_out[rnd, d] = part(lax.rem(z + d, nz), 1 - y).astype(jnp.bfloat16)
            y_copy(rnd, d).start()

        @pl.loop(1, nz)
        def _(d):
            mine = part(lax.rem(z + d, nz), y)
            y_copy(rnd, d).wait_recv()
            z_out[rnd, d] = (mine + y_in[rnd, d].astype(jnp.float32)).astype(jnp.bfloat16)
            z_copy(rnd, d).start()

        total = part(z, y)
        y_copy(rnd, 0).wait_recv()
        total = total + y_in[rnd, 0].astype(jnp.float32)
        finish(functools.partial(z_copy, rnd), nz)
        for d in range(1, nz):
            total = total + z_in[rnd, d].astype(jnp.float32)

        @pl.loop(0, nz)
        def _(d):
            y_copy(rnd, d).wait_send()

        return total

    def spread(rnd):
        v_all[rnd, rows_of(z, y)] = r_p[...].astype(jnp.bfloat16)
        pass_on(rnd, z)

    def dot(a, b):
        return jnp.sum(a * b, axis=1, keepdims=True)

    predicted = sum_rows(0)
    valid_count = sum_scalars(0)[0:1, 0:1]
    weight = mask / valid_count
    y_r = weight * (targ[...] - predicted)
    r_p[...] = pull_back(0, y_r)
    spread(0)
    t_r = tangent(0)
    wt = weight * t_r
    send_scalars(1, [dot(y_r, t_r), dot(wt, t_r)])
    q_p[...] = pull_back(1, wt)
    sums = sum_scalars(1)
    norm, curve = sums[0:1, 0:1], sums[1:2, 0:1]
    length = norm
    step = norm / (curve + damping * length)
    d_p[...] = r_p[...]
    r_p[...] = r_p[...] - step * (q_p[...] + damping * d_p[...])
    spread(1)
    t_d, y_d = t_r, y_r
    change = step * t_d
    y_r = y_r - step * (wt + damping * y_d)

    t_r = tangent(1)
    wt = weight * t_r
    send_scalars(2, [dot(y_r, t_r), dot(wt, t_r), dot(wt, t_d), dot(y_r, t_d)])
    back = pull_back(2, wt)
    sums = sum_scalars(2)
    beta = sums[0:1, 0:1] / norm
    norm = sums[0:1, 0:1]
    curve = sums[1:2, 0:1] + beta * (2.0 * sums[2:3, 0:1] + beta * curve)
    length = norm + beta * (2.0 * sums[3:4, 0:1] + beta * length)
    step = norm / (curve + damping * length)
    r_p[...] = r_p[...] - step * (
        back + beta * q_p[...] + damping * (r_p[...] + beta * d_p[...])
    )
    spread(2)
    t_d = t_r + beta * t_d
    y_d = y_r + beta * y_d
    change = change + step * t_d
    y_r = y_r - step * (weight * t_d + damping * y_d)

    t_r = tangent(2)
    wt = weight * t_r
    send_scalars(3, [dot(y_r, t_r), dot(wt, t_r), dot(wt, t_d), dot(y_r, t_d)])
    sums = sum_scalars(3)
    beta = sums[0:1, 0:1] / norm
    norm = sums[0:1, 0:1]
    curve = sums[1:2, 0:1] + beta * (2.0 * sums[2:3, 0:1] + beta * curve)
    length = norm + beta * (2.0 * sums[3:4, 0:1] + beta * length)
    step = norm / (curve + damping * length)
    t_d = t_r + beta * t_d
    out[...] = change + step * t_d


def shards(nd, nm, features_in, w_in, w_mid, w_out, targets, valid_steps):
    hidden, cols = w_mid.shape
    rows = features_in.shape[1]
    piece = hidden // nd
    vmem = pl.BlockSpec(memory_space=pltpu.VMEM)
    dma = pltpu.SemaphoreType.DMA
    bf16, f32 = jnp.bfloat16, jnp.float32
    change = pl.pallas_call(
        functools.partial(kernel, nd, nm),
        out_shape=jax.ShapeDtypeStruct((1, rows), f32),
        in_specs=[vmem] * 6,
        out_specs=vmem,
        scratch_shapes=[
            pltpu.VMEM((nm,) + w_in.shape, bf16),
            pltpu.VMEM((hidden, w_in.shape[0]), bf16),
            pltpu.VMEM((hidden, rows), bf16),
            pltpu.VMEM((cols, rows), f32),
            pltpu.VMEM((cols, rows), bf16),
            pltpu.VMEM((1, rows), f32),
            pltpu.VMEM((cols, hidden), bf16),
            pltpu.VMEM((cols, hidden), bf16),
            pltpu.VMEM((4, 1, rows), f32),
            pltpu.VMEM((4, nm, 1, rows), f32),
            pltpu.VMEM((4, 8, 128), f32),
            pltpu.VMEM((4, nd, 8, 128), f32),
            pltpu.VMEM((3, nd // 2, piece, cols), bf16),
            pltpu.VMEM((3, nd // 2, piece, cols), bf16),
            pltpu.VMEM((3, nd // 2, piece, cols), bf16),
            pltpu.VMEM((3, nd // 2, piece, cols), bf16),
            pltpu.VMEM((3, hidden, cols), bf16),
            pltpu.VMEM((piece, cols), f32),
            pltpu.VMEM((piece, cols), f32),
            pltpu.VMEM((piece, cols), f32),
            dma((nm,)), dma((nm,)),
            dma((4, nm)), dma((4, nm)),
            dma((4, nd)), dma((4, nd)),
            dma((3, nd // 2)), dma((3, nd // 2)),
            dma((3, nd // 2)), dma((3, nd // 2)),
            dma((3, nd // 2)), dma((3, nd // 2)),
            dma((3, 2, nd // 2)), dma((3, 2, nd // 2)),
        ],
        compiler_params=pltpu.CompilerParams(
            collective_id=0, has_side_effects=True, vmem_limit_bytes=56 * 1024 * 1024
        ),
    )(
        features_in,
        w_in,
        w_mid,
        w_out.reshape(1, cols),
        targets.reshape(1, rows),
        valid_steps.reshape(1, -1),
    )
    return change.reshape(rows)


def solution(mesh):
    return jax.shard_map(
        functools.partial(shards, mesh.shape["dp"], mesh.shape["mp"]),
        mesh=mesh,
        in_specs=(P(None, "dp"), P(None, "mp"), P(None, "mp"), P("mp"), P("dp"), P("dp")),
        out_specs=P("dp"),
        check_vma=False,
    )
```
